128 devices in a mesh: rep: 16 (over z, x_lo, core), tp: 8 (over y, x_hi).
Axes of the slice: x: 4 (x_hi: 2, x_lo: 2; x = x_hi * 2 + x_lo), y: 4, z: 4, core: 2. Of those that a mesh axis runs over, the one named last changes fastest.
Arguments:
- tokens_x: bfloat16 [512, 2, 8192], P('tp', None, 'rep'), may hold values from -6 to 6
- slot_rows: int32 [512], replicated, may hold values from 0 to 511, each once
- cache_keys: bfloat16 [512, 8, 384, 128], P('rep', 'tp'), may hold values from -460 to 460
- cache_values: bfloat16 [512, 8, 384, 128], P('rep', 'tp'), may hold values from -48 to 48
- lengths: int32 [512], P('rep'), may hold values from 2 to 384, as said below
- master_query: float32 [8192, 4096], P('rep', 'tp'), may hold values from -0.0625 to 0.0625
- moment_query: float32 [8192, 4096], P('rep', 'tp'), may hold values from -6 to 6
- second_query: float32 [8192, 4096], P('rep', 'tp'), may hold values from 0.1 to 10
- gradient_query: bfloat16 [8192, 4096], P('rep', 'tp'), may hold values from -6 to 6
- master_keyval: float32 [8192, 2, 1024], P('rep', None, 'tp'), may hold values from -0.0625 to 0.0625
- moment_keyval: float32 [8192, 2, 1024], P('rep', None, 'tp'), may hold values from -6 to 6
- second_keyval: float32 [8192, 2, 1024], P('rep', None, 'tp'), may hold values from 0.1 to 10
- gradient_keyval: bfloat16 [8192, 2, 1024], P('rep', None, 'tp'), may hold values from -6 to 6
- master_output: float32 [4096, 8192], P('tp', 'rep'), may hold values from -0.375 to 0.375
- moment_output: float32 [4096, 8192], P('tp', 'rep'), may hold values from -6 to 6
- second_output: float32 [4096, 8192], P('tp', 'rep'), may hold values from 0.1 to 10
- gradient_output: bfloat16 [4096, 8192], P('tp', 'rep'), may hold values from -6 to 6
Outputs:
- new_master_query: float32 [8192, 4096], P('rep', 'tp')
- new_moment_query: float32 [8192, 4096], P('rep', 'tp')
- new_second_query: float32 [8192, 4096], P('rep', 'tp')
- new_master_keyval: float32 [8192, 2, 1024], P('rep', None, 'tp')
- new_moment_keyval: float32 [8192, 2, 1024], P('rep', None, 'tp')
- new_second_keyval: float32 [8192, 2, 1024], P('rep', None, 'tp')
- new_master_output: float32 [4096, 8192], P('tp', 'rep')
- new_moment_output: float32 [4096, 8192], P('tp', 'rep')
- new_second_output: float32 [4096, 8192], P('tp', 'rep')
- decoded: bfloat16 [512, 2, 8192], P('rep', None, 'tp')
The draws below stay inside these ranges and needn't reach their ends.
Inputs may be any that keep to these rules, and one draw needn't show every extreme that they name: `slot_rows`: a permutation of the rows. `lengths`: some slot has exactly 384.
All inputs are finite; a program needn't handle non-finite values.
Results may differ from the reference program's by a relative error of at most 0.017.
Values may be sent and summed in bfloat16 or wider, within the bound.
No kernel may reach another device: no remote copies, remote signals or barrier semaphores. Data moves between devices by JAX's collectives and lax.ppermute only.
A program may use at most 320 MiB of HBM per device.

```python
import math
import jax
import jax.numpy as jnp
from jax import lax

D = 8192
QH = 32
KVH = 8
HS = 128
CACHE = 384
STEPS = 2
ROWS_REP = 32
ROWS = 512
QW = 4096
KW = 1024


def draw_cache_keys(key, part):
    key = jax.random.fold_in(key, 11)
    key_base = jax.random.fold_in(key, 0)
    shape = (ROWS, KVH, CACHE, HS)
    drawn = jnp.clip(jax.random.normal(key_base, shape, jnp.float32), -6.0, 6.0) * 1.5
    return drawn.astype(jnp.bfloat16)


def draw_lengths(key, part):
    key = jax.random.fold_in(key, 12)
    key_len, key_spot = jax.random.split(key, 2)
    filled = jax.random.randint(key_len, (ROWS,), 2, CACHE + 1, dtype=jnp.int32)
    spot = jax.random.randint(key_spot, (), 0, ROWS, dtype=jnp.int32)
    return jnp.where(jnp.arange(ROWS, dtype=jnp.int32) == spot, CACHE, filled).astype(jnp.int32)


def block_scale(stream_key, dims, shards, low, top_value):
    def one(position, shards_of):
        steps = jax.random.uniform(jax.random.fold_in(jax.random.fold_in(stream_key, 6), position), (shards_of,), jnp.float32, low / len(shards), top_value / len(shards))
        return jnp.repeat(jnp.exp(steps), dims[position] // shards_of).reshape((-1,) + (1,) * (len(dims) - position - 1))

    gain = one(*shards[0])
    for cut in shards[1:]:
        gain = gain * one(*cut)
    return gain


def gaussian(key, dims, scale, reach, pieces=(), kind=jnp.bfloat16):
    drawn = jax.random.normal(key, dims, jnp.float32) * scale
    if len(pieces) > 0:
        drawn = block_scale(key, dims, pieces, -0.22, 0.18) * drawn
    return jnp.clip(drawn, min=-reach, max=reach).astype(kind)


def setup_inputs(seed: int = 0) -> dict:
    key_list = jax.random.split(jax.random.key(seed), 18)
    tokens_x = gaussian(key_list[0], (ROWS, STEPS, D), 1.0, 6.0, ((0, 8), (2, 16)))
    slot_rows = jax.random.permutation(key_list[1], ROWS).astype(jnp.int32)
    cache_keys = draw_cache_keys(jax.random.fold_in(key_list[17], 71), 0)
    cache_values = gaussian(key_list[3], (ROWS, KVH, CACHE, HS), 8.0, 48.0, ((0, 16), (1, 8)))
    lengths = draw_lengths(jax.random.fold_in(key_list[17], 71), 0)
    master_query = gaussian(key_list[5], (D, QW), D ** -0.5, 0.0625, ((0, 16), (1, 8)), jnp.float32)
    moment_query = gaussian(key_list[6], (D, QW), 1.0, 6.0, ((0, 16), (1, 8)), jnp.float32)
    second_query = jnp.clip(jnp.exp(math.log(10.0) - 4.6051702 * jax.random.uniform(key_list[7], (D, QW), jnp.float32) ** block_scale(key_list[7], (D, QW), ((0, 16), (1, 8)), -0.2, 0.2)), 0.1, 10.0)
    gradient_query = gaussian(key_list[8], (D, QW), 1.0, 6.0, ((0, 16), (1, 8)))
    master_keyval = gaussian(key_list[9], (D, 2, KW), D ** -0.5, 0.0625, ((0, 16), (2, 8)), jnp.float32)
    moment_keyval = gaussian(key_list[10], (D, 2, KW), 1.0, 6.0, ((0, 16), (2, 8)), jnp.float32)
    second_keyval = jnp.clip(jnp.exp(math.log(10.0) - 4.6051702 * jax.random.uniform(key_list[11], (D, 2, KW), jnp.float32) ** block_scale(key_list[11], (D, 2, KW), ((0, 16), (2, 8)), -0.2, 0.2)), 0.1, 10.0)
    gradient_keyval = gaussian(key_list[12], (D, 2, KW), 1.0, 6.0, ((0, 16), (2, 8)))
    master_output = gaussian(key_list[13], (QW, D), (QW // 16) ** -0.5, 0.375, ((0, 8), (1, 16)), jnp.float32)
    moment_output = gaussian(key_list[14], (QW, D), 1.0, 6.0, ((0, 8), (1, 16)), jnp.float32)
    second_output = jnp.clip(jnp.exp(math.log(10.0) - 4.6051702 * jax.random.uniform(key_list[15], (QW, D), jnp.float32) ** block_scale(key_list[15], (QW, D), ((0, 8), (1, 16)), -0.2, 0.2)), 0.1, 10.0)
    gradient_output = gaussian(key_list[16], (QW, D), 1.0, 6.0, ((0, 8), (1, 16)))
    return dict(tokens_x=tokens_x, slot_rows=slot_rows, cache_keys=cache_keys, cache_values=cache_values, lengths=lengths, master_query=master_query, moment_query=moment_query, second_query=second_query, gradient_query=gradient_query, master_keyval=master_keyval, moment_keyval=moment_keyval, second_keyval=second_keyval, gradient_keyval=gradient_keyval, master_output=master_output, moment_output=moment_output, second_output=second_output, gradient_output=gradient_output)


learn_rate = 0.002
beta_one = 0.9
beta_two = 0.95
adam_eps = 1e-08
weight_decay = 0.1
step_count = 100.0
rope_base = 500000.0

def adam_step(master, moment, second, gradient):
    grad_wide = gradient.astype(jnp.float32)
    new_moment = beta_one * moment + (1.0 - beta_one) * grad_wide
    new_second = beta_two * second + (1.0 - beta_two) * grad_wide * grad_wide
    moment_hat = new_moment / (1.0 - beta_one ** step_count)
    second_hat = new_second / (1.0 - beta_two ** step_count)
    new_master = master - learn_rate * (moment_hat / (jnp.sqrt(second_hat) + adam_eps) + weight_decay * master)
    return (new_master, new_moment, new_second)

def rotate(vectors, positions):
    head_size = vectors.shape[-1]
    half = head_size // 2
    freqs = rope_base ** (-2.0 * jnp.arange(half, dtype=jnp.float32) / head_size)
    angles = positions[:, :, None, None].astype(jnp.float32) * freqs
    cosine = jnp.cos(angles)
    sine = jnp.sin(angles)
    first = vectors[..., :half]
    latter = vectors[..., half:]
    return jnp.concatenate([first * cosine - latter * sine, latter * cosine + first * sine], axis=-1)

def attend_block(operands):
    q_rot, k_new, v_new, keys, values, lengths = operands
    rows, steps, heads, head_size = q_rot.shape
    key_heads = keys.shape[1]
    group = heads // key_heads
    cache = keys.shape[2]
    q_five = q_rot.astype(jnp.float32).reshape(rows, steps, key_heads, group, head_size)
    scale = 1.0 / head_size ** 0.5
    hp = lax.Precision.HIGHEST
    old_scores = jnp.einsum('rskgd,rkcd->rskgc', q_five, keys.astype(jnp.float32), precision=hp) * scale
    new_scores = jnp.einsum('rskgd,rjkd->rskgj', q_five, k_new.astype(jnp.float32), precision=hp) * scale
    valid = jnp.arange(cache, dtype=jnp.int32)[None, :] < lengths[:, None]
    old_scores = jnp.where(valid[:, None, None, None, :], old_scores, -1e+30)
    causal = jnp.arange(steps, dtype=jnp.int32)[None, :] <= jnp.arange(steps, dtype=jnp.int32)[:, None]
    new_scores = jnp.where(causal[None, :, None, None, :], new_scores, -1e+30)
    top = jnp.maximum(lax.optimization_barrier(jnp.max(old_scores, axis=-1, keepdims=True)), lax.optimization_barrier(jnp.max(new_scores, axis=-1, keepdims=True)))
    exp_old = jnp.exp(old_scores - top)
    exp_new = jnp.exp(new_scores - top)
    total = lax.optimization_barrier(jnp.sum(exp_old, axis=-1, keepdims=True)) + lax.optimization_barrier(jnp.sum(exp_new, axis=-1, keepdims=True))
    weight_old = (exp_old / total).astype(jnp.bfloat16).astype(jnp.float32)
    weight_new = (exp_new / total).astype(jnp.bfloat16).astype(jnp.float32)
    mixed = jnp.einsum('rskgc,rkcd->rskgd', weight_old, values.astype(jnp.float32), precision=hp)
    mixed = mixed + jnp.einsum('rskgj,rjkd->rskgd', weight_new, v_new.astype(jnp.float32), precision=hp)
    return mixed.reshape(rows, steps, heads * head_size).astype(jnp.bfloat16)

def reference(tokens_x, slot_rows, cache_keys, cache_values, lengths, master_query, moment_query, second_query, gradient_query, master_keyval, moment_keyval, second_keyval, gradient_keyval, master_output, moment_output, second_output, gradient_output):
    state_query = adam_step(master_query, moment_query, second_query, gradient_query)
    state_keyval = adam_step(master_keyval, moment_keyval, second_keyval, gradient_keyval)
    state_output = adam_step(master_output, moment_output, second_output, gradient_output)
    w_query = state_query[0].astype(jnp.bfloat16)
    w_keyval = state_keyval[0].astype(jnp.bfloat16).reshape(D, 2 * KW)
    w_output = state_output[0].astype(jnp.bfloat16)
    ordered = jnp.take(tokens_x, slot_rows, axis=0)
    flat_rows = ordered.reshape(ROWS * STEPS, D)
    query = jnp.dot(flat_rows, w_query, preferred_element_type=jnp.float32).reshape(ROWS, STEPS, QH, HS)
    keyval = jnp.dot(flat_rows, w_keyval, preferred_element_type=jnp.float32).reshape(ROWS, STEPS, 2, KVH, HS)
    positions = lengths[:, None] + jnp.arange(STEPS, dtype=jnp.int32)[None, :]
    q_rot = rotate(query, positions).astype(jnp.bfloat16)
    k_new = rotate(keyval[:, :, 0], positions).astype(jnp.bfloat16)
    v_new = keyval[:, :, 1].astype(jnp.bfloat16)
    blocks = ROWS // ROWS_REP
    operands = (q_rot.reshape(blocks, ROWS_REP, STEPS, QH, HS), k_new.reshape(blocks, ROWS_REP, STEPS, KVH, HS), v_new.reshape(blocks, ROWS_REP, STEPS, KVH, HS), cache_keys.reshape(blocks, ROWS_REP, KVH, CACHE, HS), cache_values.reshape(blocks, ROWS_REP, KVH, CACHE, HS), lengths.reshape(blocks, ROWS_REP))
    attended = lax.map(attend_block, operands).reshape(ROWS * STEPS, QW)
    decoded = jnp.dot(attended, w_output, preferred_element_type=jnp.float32).astype(jnp.bfloat16).reshape(ROWS, STEPS, D)
    return (state_query[0], state_query[1], state_query[2], state_keyval[0], state_keyval[1], state_keyval[2], state_output[0], state_output[1], state_output[2], decoded)
```

```python
import functools

import jax
import jax.numpy as jnp
from jax import lax
from jax.experimental import pallas as pl
from jax.experimental.pallas import tpu as pltpu
from jax.sharding import Mesh, PartitionSpec as P

learn_rate = 0.002
beta_one = 0.9
beta_two = 0.95
adam_eps = 1e-08
weight_decay = 0.1
step_count = 100.0
rope_base = 500000.0

AXES = ("z", "xl", "c", "y", "xh")
SIZES = (4, 2, 2, 4, 2)
CHIPS = ("z", "xl")
TP = ("y", "xh")
STEPS = 2
SLOTS = 32
CACHE = 384
HEAD = 128
GROUP = 4
MIB = 1024 * 1024


def adam_step(master, moment, second, gradient):
    grad_wide = gradient.astype(jnp.float32)
    new_moment = beta_one * moment + (1.0 - beta_one) * grad_wide
    new_second = beta_two * second + (1.0 - beta_two) * grad_wide * grad_wide
    moment_hat = new_moment / (1.0 - beta_one**step_count)
    second_hat = new_second / (1.0 - beta_two**step_count)
    new_master = master - learn_rate * (
        moment_hat / (jnp.sqrt(second_hat) + adam_eps) + weight_decay * master
    )
    return (new_master, new_moment, new_second)


def move(array, target):
    pairs = []
    for source in range(128):
        rest, coords = source, []
        for size in reversed(SIZES):
            rest, coord = divmod(rest, size)
            coords.append(coord)
        index = 0
        for coord, size in zip(target(*reversed(coords)), SIZES):
            index = index * size + coord % size
        pairs.append((source, index))
    return lax.ppermute(array, AXES, pairs)


def to_sibling(array):
    return move(array, lambda z, xl, c, y, xh: (z, xl, 1 - c, y, xh))


def dot(a, b):
    return jnp.dot(a, b, preferred_element_type=jnp.float32)


def params(mib):
    return pltpu.CompilerParams(vmem_limit_bytes=mib * MIB)


VMEM = pl.BlockSpec(memory_space=pltpu.VMEM)
SMEM = pl.BlockSpec(memory_space=pltpu.SMEM)
ANY = pl.BlockSpec(memory_space=pl.ANY)


def select_rows(slots, rows):
    hot = lax.broadcasted_iota(jnp.int32, (slots.shape[0], rows), 1) == slots
    return hot.astype(jnp.bfloat16)


def order_kernel(slots_ref, x_ref, out_ref):
    hot = select_rows(slots_ref[...], x_ref.shape[0])
    out_ref[...] = dot(hot, x_ref[...]).astype(jnp.bfloat16)


def own_kernel(slots_ref, x_ref, w_ref, out_ref):
    hot = select_rows(slots_ref[...], x_ref.shape[0])
    half = x_ref.shape[1] // STEPS
    for step in range(STEPS):
        ordered = dot(hot, x_ref[:, step * half : (step + 1) * half]).astype(jnp.bfloat16)
        out_ref[step] = dot(ordered, w_ref[...])


def add_kernel(own_ref, x_ref, w_ref, out_ref):
    half = x_ref.shape[1] // STEPS
    for step in range(STEPS):
        total = own_ref[step] + dot(x_ref[:, step * half : (step + 1) * half], w_ref[...])
        total = total.astype(jnp.bfloat16)
        for chip in range(8):
            out_ref[chip, step * SLOTS : (step + 1) * SLOTS, :] = total[
                chip * SLOTS : (chip + 1) * SLOTS
            ]


CHUNKS = 4
PER = SLOTS // CHUNKS
ROWS = STEPS * GROUP


def attend_kernel(
    parts_ref, cos_ref, sin_ref, len_ref, keys_ref, values_ref, out_ref,
    key_buf, value_buf, q_buf, kx_buf, vx_buf, mix_buf, att_buf, key_sem, value_sem,
):
    copies = []
    for chunk in range(CHUNKS):
        rows = pl.ds(chunk * PER, PER)
        for source, buf, sem in (
            (keys_ref, key_buf, key_sem),
            (values_ref, value_buf, value_sem),
        ):
            copy = pltpu.make_async_copy(source.at[rows], buf.at[rows], sem.at[chunk])
            copy.start()
            copies.append(copy)
    total = parts_ref[0].astype(jnp.float32)
    for chip in range(1, 8):
        total = total + parts_ref[chip].astype(jnp.float32)
    cosine = cos_ref[...]
    sine = sin_ref[...]

    def rotate(vectors):
        turned = vectors * cosine + pltpu.roll(vectors, HEAD // 2, 1) * sine
        return turned.astype(jnp.bfloat16).astype(jnp.float32)

    for head in range(GROUP):
        turned = rotate(total[:, head * HEAD : (head + 1) * HEAD])
        for step in range(STEPS):
            q_buf[pl.ds(step * GROUP + head, SLOTS, stride=ROWS), :] = turned[
                step * SLOTS : (step + 1) * SLOTS
            ]
    k_new = rotate(total[:, GROUP * HEAD : (GROUP + 1) * HEAD])
    v_new = total[:, (GROUP + 1) * HEAD :].astype(jnp.bfloat16).astype(jnp.float32)
    for step in range(STEPS):
        for row in range(ROWS):
            kx_buf[step, pl.ds(row, SLOTS, stride=ROWS), :] = k_new[
                step * SLOTS : (step + 1) * SLOTS
            ]
            vx_buf[step, pl.ds(row, SLOTS, stride=ROWS), :] = v_new[
                step * SLOTS : (step + 1) * SLOTS
            ]
    scale = 1.0 / HEAD**0.5
    many = PER * ROWS
    for chunk in range(CHUNKS):
        first = chunk * many
        q_rows = q_buf[first : first + many]
        new_zero = jnp.sum(q_rows * kx_buf[0, first : first + many], axis=-1, keepdims=True) * scale
        new_one = jnp.sum(q_rows * kx_buf[1, first : first + many], axis=-1, keepdims=True) * scale
        row = lax.broadcasted_iota(jnp.int32, (many, 1), 0)
        second_step = lax.rem(row, ROWS) >= GROUP
        new_one = jnp.where(second_step, new_one, -1e30)
        copies[2 * chunk].wait()
        scores = []
        for slot in range(PER):
            scores.append(
                lax.dot_general(
                    q_rows[slot * ROWS : (slot + 1) * ROWS].astype(jnp.bfloat16),
                    key_buf[chunk * PER + slot],
                    (((1,), (1,)), ((), ())),
                    preferred_element_type=jnp.float32,
                )
            )
        scores = jnp.concatenate(scores, axis=0) * scale
        position = lax.broadcasted_iota(jnp.int32, (many, CACHE), 1)
        scores = jnp.where(position < len_ref[first : first + many], scores, -1e30)
        top = jnp.maximum(
            jnp.max(scores, axis=-1, keepdims=True), jnp.maximum(new_zero, new_one)
        )
        scores = jnp.exp(scores - top)
        new_zero = jnp.exp(new_zero - top)
        new_one = jnp.exp(new_one - top)
        total_exp = jnp.sum(scores, axis=-1, keepdims=True) + new_zero + new_one
        scores = scores / total_exp
        new_zero = (new_zero / total_exp).astype(jnp.bfloat16).astype(jnp.float32)
        new_one = (new_one / total_exp).astype(jnp.bfloat16).astype(jnp.float32)
        copies[2 * chunk + 1].wait()
        mixed = []
        for slot in range(PER):
            mixed.append(
                dot(
                    scores[slot * ROWS : (slot + 1) * ROWS].astype(jnp.bfloat16),
                    value_buf[chunk * PER + slot],
                )
            )
        mixed = jnp.concatenate(mixed, axis=0)
        mixed = mixed + new_zero * vx_buf[0, first : first + many]
        mixed = mixed + new_one * vx_buf[1, first : first + many]
        mix_buf[first : first + many] = mixed
    for head in range(GROUP):
        for step in range(STEPS):
            att_buf[head, pl.ds(step, SLOTS, stride=STEPS), :] = mix_buf[
                pl.ds(step * GROUP + head, SLOTS, stride=ROWS), :
            ]
    for core in range(2):
        for head in range(2):
            part = att_buf[core * 2 + head].astype(jnp.bfloat16)
            for chip in range(8):
                out_ref[core * 8 + chip, :, head * HEAD : (head + 1) * HEAD] = part


def attend(parts, cosine, sine, lengths, keys, values):
    flat = SLOTS * ROWS
    return pl.pallas_call(
        attend_kernel,
        out_shape=jax.ShapeDtypeStruct((16, STEPS * SLOTS, 2 * HEAD), jnp.bfloat16),
        in_specs=[VMEM, VMEM, VMEM, VMEM, ANY, ANY],
        out_specs=VMEM,
        scratch_shapes=[
            pltpu.VMEM((SLOTS, CACHE, HEAD), jnp.bfloat16),
            pltpu.VMEM((SLOTS, CACHE, HEAD), jnp.bfloat16),
            pltpu.VMEM((flat, HEAD), jnp.float32),
            pltpu.VMEM((STEPS, flat, HEAD), jnp.float32),
            pltpu.VMEM((STEPS, flat, HEAD), jnp.float32),
            pltpu.VMEM((flat, HEAD), jnp.float32),
            pltpu.VMEM((GROUP, STEPS * SLOTS, HEAD), jnp.float32),
            pltpu.SemaphoreType.DMA((CHUNKS,)),
            pltpu.SemaphoreType.DMA((CHUNKS,)),
        ],
        compiler_params=params(32),
    )(parts, cosine, sine, lengths, keys, values)


def out_kernel(att_ref, w_ref, out_ref):
    @pl.when(pl.program_id(0) == 0)
    def _():
        out_ref[...] = jnp.zeros_like(out_ref)

    for core in range(2):
        total = out_ref[core]
        for part in range(2):
            total = total + dot(att_ref[core, part], w_ref[part])
        out_ref[core] = total


def project(att, w_all):
    return pl.pallas_call(
        out_kernel,
        grid=(4,),
        out_shape=jax.ShapeDtypeStruct((2, 64, 1024), jnp.float32),
        in_specs=[
            pl.BlockSpec((2, 2, 64, 256), lambda i: (0, i, 0, 0)),
            pl.BlockSpec((2, 256, 1024), lambda i: (i, 0, 0)),
        ],
        out_specs=pl.BlockSpec((2, 64, 1024), lambda i: (0, 0, 0)),
        compiler_params=params(16),
    )(att, w_all)


def per_device(
    tokens_x,
    slot_rows,
    cache_keys,
    cache_values,
    lengths,
    master_query,
    moment_query,
    second_query,
    gradient_query,
    master_keyval,
    moment_keyval,
    second_keyval,
    gradient_keyval,
    master_output,
    moment_output,
    second_output,
    gradient_output,
):
    core = lax.axis_index("c")

    x_own = tokens_x.reshape(64, 1024)
    x_all = lax.all_to_all(
        jnp.broadcast_to(x_own[None], (8, 64, 1024)), TP, 0, 0, tiled=True
    ).reshape(512, 1024)

    state_output = adam_step(master_output, moment_output, second_output, gradient_output)
    w_output = state_output[0].astype(jnp.bfloat16)
    halves = w_output.reshape(2, 256, 512)
    w_keep = move(
        lax.dynamic_index_in_dim(halves, core, 0, False),
        lambda z, xl, c, y, xh: (y, xh, c, z, xl),
    )
    w_cross = move(
        lax.dynamic_index_in_dim(halves, 1 - core, 0, False),
        lambda z, xl, c, y, xh: (y, xh, 1 - c, z, xl),
    )
    w_wide = jnp.where(
        core == 0,
        jnp.concatenate([w_keep, w_cross], axis=1),
        jnp.concatenate([w_cross, w_keep], axis=1),
    )
    w_all = lax.all_gather(w_wide, CHIPS, axis=0)

    state_query = adam_step(master_query, moment_query, second_query, gradient_query)
    state_keyval = adam_step(master_keyval, moment_keyval, second_keyval, gradient_keyval)
    w_own = jnp.concatenate(
        [
            state_query[0].astype(jnp.bfloat16),
            state_keyval[0].astype(jnp.bfloat16).reshape(512, 256),
        ],
        axis=1,
    )
    w_sibling = to_sibling(w_own)

    by_core = slot_rows.reshape(8, 2, SLOTS).transpose(1, 0, 2).reshape(2, 256, 1)
    mine = lax.dynamic_index_in_dim(by_core, core, 0, False)
    others = lax.dynamic_index_in_dim(by_core, 1 - core, 0, False)
    x_send = pl.pallas_call(
        order_kernel,
        out_shape=jax.ShapeDtypeStruct((256, 1024), jnp.bfloat16),
        in_specs=[VMEM] * 2,
        out_specs=VMEM,
        compiler_params=params(16),
    )(others, x_all)
    x_sibling = to_sibling(x_send)
    own = pl.pallas_call(
        own_kernel,
        out_shape=jax.ShapeDtypeStruct((STEPS, 256, 768), jnp.float32),
        in_specs=[VMEM] * 3,
        out_specs=VMEM,
        compiler_params=params(16),
    )(mine, x_all, w_own)
    parts = pl.pallas_call(
        add_kernel,
        out_shape=jax.ShapeDtypeStruct((8, STEPS * SLOTS, 768), jnp.bfloat16),
        in_specs=[VMEM] * 3,
        out_specs=VMEM,
        compiler_params=params(16),
    )(own, x_sibling, w_sibling)
    parts = lax.all_to_all(parts, CHIPS, 0, 0, tiled=True)

    positions = (
        jnp.arange(STEPS, dtype=jnp.int32)[:, None] + lengths[None, :]
    ).reshape(STEPS * SLOTS, 1)
    freqs = rope_base ** (-2.0 * jnp.arange(HEAD // 2, dtype=jnp.float32) / HEAD)
    angles = positions.astype(jnp.float32) * freqs
    cosine = jnp.cos(angles)
    sine = jnp.sin(angles)
    cosine = jnp.concatenate([cosine, cosine], axis=1)
    sine = jnp.concatenate([-sine, sine], axis=1)
    attended = attend(
        parts,
        cosine,
        sine,
        jnp.repeat(lengths, ROWS)[:, None],
        cache_keys.reshape(SLOTS, CACHE, HEAD),
        cache_values.reshape(SLOTS, CACHE, HEAD),
    )
    attended = lax.all_to_all(attended, ("c",) + TP, 0, 0, tiled=True)
    partial_out = project(attended.reshape(2, 8, 64, 256), w_all)
    arrived = to_sibling(lax.dynamic_index_in_dim(partial_out, 1 - core, 0, False))
    decoded = lax.dynamic_index_in_dim(partial_out, core, 0, False) + arrived
    decoded = decoded.astype(jnp.bfloat16).reshape(SLOTS, STEPS, 1024)
    return (
        state_query[0],
        state_query[1],
        state_query[2],
        state_keyval[0],
        state_keyval[1],
        state_keyval[2],
        state_output[0],
        state_output[1],
        state_output[2],
        decoded,
    )


def solution(mesh):
    fine = Mesh(mesh.devices.reshape(SIZES), AXES)
    rep = ("z", "xl", "c")
    tp = TP
    return jax.shard_map(
        per_device,
        mesh=fine,
        in_specs=(
            P(tp, None, rep),
            P(),
            P(rep, tp, None, None),
            P(rep, tp, None, None),
            P(rep),
            P(rep, tp),
            P(rep, tp),
            P(rep, tp),
            P(rep, tp),
            P(rep, None, tp),
            P(rep, None, tp),
            P(rep, None, tp),
            P(rep, None, tp),
            P(tp, rep),
            P(tp, rep),
            P(tp, rep),
            P(tp, rep),
        ),
        out_specs=(
            P(rep, tp),
            P(rep, tp),
            P(rep, tp),
            P(rep, None, tp),
            P(rep, None, tp),
            P(rep, None, tp),
            P(tp, rep),
            P(tp, rep),
            P(tp, rep),
            P(rep, None, tp),
        ),
        check_vma=False,
    )
```

```python
import functools

import jax
import jax.numpy as jnp
from jax import lax
from jax.experimental import pallas as pl
from jax.experimental.pallas import tpu as pltpu
from jax.sharding import Mesh, PartitionSpec as P

learn_rate = 0.002
beta_one = 0.9
beta_two = 0.95
adam_eps = 1e-08
weight_decay = 0.1
step_count = 100.0
rope_base = 500000.0

AXES = ("z", "xl", "c", "y", "xh")
SIZES = (4, 2, 2, 4, 2)
CHIPS = ("z", "xl")
TP = ("y", "xh")
STEPS = 2
SLOTS = 32
CACHE = 384
HEAD = 128
GROUP = 4
OUTPUT = 512
MIB = 1024 * 1024


def adam_step(master, moment, second, gradient):
    grad_wide = gradient.astype(jnp.float32)
    new_moment = beta_one * moment + (1.0 - beta_one) * grad_wide
    new_second = beta_two * second + (1.0 - beta_two) * grad_wide * grad_wide
    moment_hat = new_moment / (1.0 - beta_one**step_count)
    second_hat = new_second / (1.0 - beta_two**step_count)
    new_master = master - learn_rate * (
        moment_hat / (jnp.sqrt(second_hat) + adam_eps) + weight_decay * master
    )
    return (new_master, new_moment, new_second)


def move(array, target):
    pairs = []
    for source in range(128):
        rest, coords = source, []
        for size in reversed(SIZES):
            rest, coord = divmod(rest, size)
            coords.append(coord)
        index = 0
        for coord, size in zip(target(*reversed(coords)), SIZES):
            index = index * size + coord % size
        pairs.append((source, index))
    return lax.ppermute(array, AXES, pairs)


def to_sibling(array):
    return move(array, lambda z, xl, c, y, xh: (z, xl, 1 - c, y, xh))


def transpose(array):
    return move(array, lambda z, xl, c, y, xh: (y, xh, c, z, xl))


def dot(a, b):
    return jnp.dot(a, b, preferred_element_type=jnp.float32)


def params(mib):
    return pltpu.CompilerParams(vmem_limit_bytes=mib * MIB)


VMEM = pl.BlockSpec(memory_space=pltpu.VMEM)
SMEM = pl.BlockSpec(memory_space=pltpu.SMEM)
HBM = pl.BlockSpec(memory_space=pltpu.HBM)


def select_rows(slots, rows):
    hot = lax.broadcasted_iota(jnp.int32, (slots.shape[0], rows), 1) == slots
    return hot.astype(jnp.bfloat16)


def order_kernel(slots_ref, x_ref, out_ref):
    hot = select_rows(slots_ref[...], x_ref.shape[0])
    out_ref[...] = dot(hot, x_ref[...]).astype(jnp.bfloat16)


def own_kernel(slots_ref, x_ref, w_ref, out_ref):
    hot = select_rows(slots_ref[...], x_ref.shape[0])
    half = x_ref.shape[1] // STEPS
    for step in range(STEPS):
        ordered = dot(hot, x_ref[:, step * half : (step + 1) * half]).astype(jnp.bfloat16)
        out_ref[step] = dot(ordered, w_ref[:, OUTPUT:])


def add_kernel(own_ref, x_ref, w_ref, cos_ref, sin_ref, len_ref, out_ref):
    del cos_ref, sin_ref, len_ref
    half = x_ref.shape[1] // STEPS
    for step in range(STEPS):
        total = own_ref[step] + dot(x_ref[:, step * half : (step + 1) * half], w_ref[:, OUTPUT:])
        total = total.astype(jnp.bfloat16)
        for chip in range(8):
            out_ref[chip, step * SLOTS : (step + 1) * SLOTS, :] = total[
                chip * SLOTS : (chip + 1) * SLOTS
            ]


CHUNKS = 2
PER = SLOTS // CHUNKS
ROWS = STEPS * GROUP
AHEAD = 2


def attend_kernel(
    parts_ref, cos_ref, sin_ref, len_ref, keys_ref, values_ref, out_ref,
    key_buf, value_buf, q_buf, kx_buf, vx_buf, mix_buf, att_buf, key_sem, value_sem,
):
    copies = []
    for chunk in range(CHUNKS):
        rows = pl.ds(chunk * PER, PER)
        copies.append(
            (
                pltpu.make_async_copy(keys_ref.at[rows], key_buf.at[rows], key_sem.at[chunk]),
                pltpu.make_async_copy(values_ref.at[rows], value_buf.at[rows], value_sem.at[chunk]),
            )
        )
    for chunk in range(AHEAD):
        copies[chunk][0].start()
        copies[chunk][1].start()
    total = parts_ref[0].astype(jnp.float32)
    for chip in range(1, 8):
        total = total + parts_ref[chip].astype(jnp.float32)
    cosine = cos_ref[...]
    sine = sin_ref[...]

    def rotate(vectors):
        turned = vectors * cosine + pltpu.roll(vectors, HEAD // 2, 1) * sine
        return turned.astype(jnp.bfloat16).astype(jnp.float32)

    for head in range(GROUP):
        turned = rotate(total[:, head * HEAD : (head + 1) * HEAD])
        for step in range(STEPS):
            q_buf[pl.ds(step * GROUP + head, SLOTS, stride=ROWS), :] = turned[
                step * SLOTS : (step + 1) * SLOTS
            ]
    k_new = rotate(total[:, GROUP * HEAD : (GROUP + 1) * HEAD])
    v_new = total[:, (GROUP + 1) * HEAD :].astype(jnp.bfloat16).astype(jnp.float32)
    for step in range(STEPS):
        for row in range(ROWS):
            kx_buf[step, pl.ds(row, SLOTS, stride=ROWS), :] = k_new[
                step * SLOTS : (step + 1) * SLOTS
            ]
            vx_buf[step, pl.ds(row, SLOTS, stride=ROWS), :] = v_new[
                step * SLOTS : (step + 1) * SLOTS
            ]
    scale = 1.0 / HEAD**0.5
    many = PER * ROWS
    for chunk in range(CHUNKS):
        first = chunk * many
        q_rows = q_buf[first : first + many]
        new_zero = jnp.sum(q_rows * kx_buf[0, first : first + many], axis=-1, keepdims=True) * scale
        new_one = jnp.sum(q_rows * kx_buf[1, first : first + many], axis=-1, keepdims=True) * scale
        row = lax.broadcasted_iota(jnp.int32, (many, 1), 0)
        second_step = lax.rem(row, ROWS) >= GROUP
        new_one = jnp.where(second_step, new_one, -1e30)
        copies[chunk][0].wait()
        if chunk + AHEAD < CHUNKS:
            copies[chunk + AHEAD][0].start()
            copies[chunk + AHEAD][1].start()
        scores = []
        for slot in range(PER):
            scores.append(
                lax.dot_general(
                    q_rows[slot * ROWS : (slot + 1) * ROWS].astype(jnp.bfloat16),
                    key_buf[chunk * PER + slot],
                    (((1,), (1,)), ((), ())),
                    preferred_element_type=jnp.float32,
                )
            )
        scores = jnp.concatenate(scores, axis=0) * scale
        position = lax.broadcasted_iota(jnp.int32, (many, CACHE), 1)
        scores = jnp.where(position < len_ref[first : first + many], scores, -1e30)
        top = jnp.maximum(
            jnp.max(scores, axis=-1, keepdims=True), jnp.maximum(new_zero, new_one)
        )
        scores = jnp.exp(scores - top)
        new_zero = jnp.exp(new_zero - top)
        new_one = jnp.exp(new_one - top)
        total_exp = jnp.sum(scores, axis=-1, keepdims=True) + new_zero + new_one
        scores = scores / total_exp
        new_zero = (new_zero / total_exp).astype(jnp.bfloat16).astype(jnp.float32)
        new_one = (new_one / total_exp).astype(jnp.bfloat16).astype(jnp.float32)
        copies[chunk][1].wait()
        mixed = []
        for slot in range(PER):
            mixed.append(
                dot(
                    scores[slot * ROWS : (slot + 1) * ROWS].astype(jnp.bfloat16),
                    value_buf[chunk * PER + slot],
                )
            )
        mixed = jnp.concatenate(mixed, axis=0)
        mixed = mixed + new_zero * vx_buf[0, first : first + many]
        mixed = mixed + new_one * vx_buf[1, first : first + many]
        mix_buf[first : first + many] = mixed
    for head in range(GROUP):
        for step in range(STEPS):
            att_buf[head, pl.ds(step, SLOTS, stride=STEPS), :] = mix_buf[
                pl.ds(step * GROUP + head, SLOTS, stride=ROWS), :
            ]
    for head in range(GROUP):
        part = att_buf[head].astype(jnp.bfloat16)
        for chip in range(8):
            out_ref[chip, :, head * HEAD : (head + 1) * HEAD] = part


def in_hbm(array):
    return pltpu.with_memory_space_constraint(array, pltpu.HBM)


def attend(parts, cosine, sine, lengths, keys, values):
    flat = SLOTS * ROWS
    return pl.pallas_call(
        attend_kernel,
        out_shape=jax.ShapeDtypeStruct((8, STEPS * SLOTS, GROUP * HEAD), jnp.bfloat16),
        in_specs=[VMEM, VMEM, VMEM, VMEM, HBM, HBM],
        out_specs=VMEM,
        scratch_shapes=[
            pltpu.VMEM((SLOTS, CACHE, HEAD), jnp.bfloat16),
            pltpu.VMEM((SLOTS, CACHE, HEAD), jnp.bfloat16),
            pltpu.VMEM((flat, HEAD), jnp.float32),
            pltpu.VMEM((STEPS, flat, HEAD), jnp.float32),
            pltpu.VMEM((STEPS, flat, HEAD), jnp.float32),
            pltpu.VMEM((flat, HEAD), jnp.float32),
            pltpu.VMEM((GROUP, STEPS * SLOTS, HEAD), jnp.float32),
            pltpu.SemaphoreType.DMA((CHUNKS,)),
            pltpu.SemaphoreType.DMA((CHUNKS,)),
        ],
        compiler_params=params(16),
    )(parts, cosine, sine, lengths, keys, values)


def out_kernel(core_ref, att_ref, own_ref, sibling_ref, out_ref):
    core = core_ref[0]
    for w_ref, half in ((own_ref, core), (sibling_ref, 1 - core)):
        product = dot(att_ref[...], w_ref[...]).astype(jnp.bfloat16)
        columns = pl.ds(pl.multiple_of(half * 512, 512), 512)
        for chip in range(8):
            out_ref[chip, :, columns] = product[chip * 64 : (chip + 1) * 64]


def project(core, att, own, sibling):
    return pl.pallas_call(
        out_kernel,
        out_shape=jax.ShapeDtypeStruct((8, 64, 1024), jnp.bfloat16),
        grid=(1,),
        in_specs=[
            SMEM,
            pl.BlockSpec((512, 512), lambda i: (0, 0)),
            pl.BlockSpec((512, OUTPUT), lambda i: (0, 0)),
            pl.BlockSpec((512, OUTPUT), lambda i: (0, 0)),
        ],
        out_specs=pl.BlockSpec((8, 64, 1024), lambda i: (0, 0, 0)),
        compiler_params=params(16),
    )(core, att, own, sibling)


def per_device(
    tokens_x,
    slot_rows,
    cache_keys,
    cache_values,
    lengths,
    master_query,
    moment_query,
    second_query,
    gradient_query,
    master_keyval,
    moment_keyval,
    second_keyval,
    gradient_keyval,
    master_output,
    moment_output,
    second_output,
    gradient_output,
):
    core = lax.axis_index("c")

    x_own = tokens_x.reshape(64, 1024)
    x_all = lax.all_to_all(
        jnp.broadcast_to(x_own[None], (8, 64, 1024)), TP, 0, 0, tiled=True
    ).reshape(512, 1024)

    state_output = adam_step(master_output, moment_output, second_output, gradient_output)
    w_output = state_output[0].astype(jnp.bfloat16)
    state_query = adam_step(master_query, moment_query, second_query, gradient_query)
    state_keyval = adam_step(master_keyval, moment_keyval, second_keyval, gradient_keyval)
    w_own = jnp.concatenate(
        [
            w_output,
            state_query[0].astype(jnp.bfloat16),
            state_keyval[0].astype(jnp.bfloat16).reshape(512, 256),
        ],
        axis=1,
    )
    w_sibling = to_sibling(w_own)

    by_core = slot_rows.reshape(8, 2, SLOTS).transpose(1, 0, 2).reshape(2, 256, 1)
    mine = lax.dynamic_index_in_dim(by_core, core, 0, False)
    others = lax.dynamic_index_in_dim(by_core, 1 - core, 0, False)
    x_send = pl.pallas_call(
        order_kernel,
        out_shape=jax.ShapeDtypeStruct((256, 1024), jnp.bfloat16),
        in_specs=[VMEM] * 2,
        out_specs=VMEM,
        compiler_params=params(16),
    )(others, x_all)
    x_sibling = to_sibling(x_send)
    own = pl.pallas_call(
        own_kernel,
        out_shape=jax.ShapeDtypeStruct((STEPS, 256, 768), jnp.float32),
        in_specs=[VMEM] * 3,
        out_specs=VMEM,
        compiler_params=params(16),
    )(mine, x_all, w_own)
    positions = (
        jnp.arange(STEPS, dtype=jnp.int32)[:, None] + lengths[None, :]
    ).reshape(STEPS * SLOTS, 1)
    freqs = rope_base ** (-2.0 * jnp.arange(HEAD // 2, dtype=jnp.float32) / HEAD)
    angles = positions.astype(jnp.float32) * freqs
    cosine = jnp.cos(angles)
    sine = jnp.sin(angles)
    cosine = jnp.concatenate([cosine, cosine], axis=1)
    sine = jnp.concatenate([-sine, sine], axis=1)
    length_rows = jnp.repeat(lengths, ROWS)[:, None]
    parts = pl.pallas_call(
        add_kernel,
        out_shape=jax.ShapeDtypeStruct((8, STEPS * SLOTS, 768), jnp.bfloat16),
        in_specs=[VMEM] * 6,
        out_specs=VMEM,
        compiler_params=params(16),
    )(own, x_sibling, w_sibling, cosine, sine, length_rows)
    parts = lax.all_to_all(parts, CHIPS, 0, 0, tiled=True)

    attended = attend(
        parts,
        cosine,
        sine,
        length_rows,
        in_hbm(cache_keys.reshape(SLOTS, CACHE, HEAD)),
        in_hbm(cache_values.reshape(SLOTS, CACHE, HEAD)),
    )
    attended = lax.all_to_all(attended, CHIPS, 0, 0, tiled=True).reshape(512, 512)
    partial_out = project(core.reshape(1), attended, w_own, w_sibling)
    partial_out = lax.all_to_all(partial_out, TP, 0, 0, tiled=True)
    decoded = jnp.sum(partial_out.astype(jnp.float32), axis=0).astype(jnp.bfloat16)
    decoded = transpose(decoded).reshape(SLOTS, STEPS, 1024)
    return (
        state_query[0],
        state_query[1],
        state_query[2],
        state_keyval[0],
        state_keyval[1],
        state_keyval[2],
        state_output[0],
        state_output[1],
        state_output[2],
        decoded,
    )


def solution(mesh):
    fine = Mesh(mesh.devices.reshape(SIZES), AXES)
    rep = ("z", "xl", "c")
    tp = TP
    return jax.shard_map(
        per_device,
        mesh=fine,
        in_specs=(
            P(tp, None, rep),
            P(),
            P(rep, tp, None, None),
            P(rep, tp, None, None),
            P(rep),
            P(rep, tp),
            P(rep, tp),
            P(rep, tp),
            P(rep, tp),
            P(rep, None, tp),
            P(rep, None, tp),
            P(rep, None, tp),
            P(rep, None, tp),
            P(tp, rep),
            P(tp, rep),
            P(tp, rep),
            P(tp, rep),
        ),
        out_specs=(
            P(rep, tp),
            P(rep, tp),
            P(rep, tp),
            P(rep, None, tp),
            P(rep, None, tp),
            P(rep, None, tp),
            P(tp, rep),
            P(tp, rep),
            P(tp, rep),
            P(rep, None, tp),
        ),
        check_vma=False,
    )
```

```python
import functools

import jax
import jax.numpy as jnp
from jax import lax
from jax.experimental import pallas as pl
from jax.experimental.pallas import tpu as pltpu
from jax.sharding import Mesh, PartitionSpec as P

learn_rate = 0.002
beta_one = 0.9
beta_two = 0.95
adam_eps = 1e-08
weight_decay = 0.1
step_count = 100.0
rope_base = 500000.0

AXES = ("z", "xl", "c", "y", "xh")
SIZES = (4, 2, 2, 4, 2)
CHIPS = ("z", "xl")
TP = ("y", "xh")
STEPS = 2
SLOTS = 32
CACHE = 384
HEAD = 128
GROUP = 4
MIB = 1024 * 1024


def adam_step(master, moment, second, gradient):
    grad_wide = gradient.astype(jnp.float32)
    new_moment = beta_one * moment + (1.0 - beta_one) * grad_wide
    new_second = beta_two * second + (1.0 - beta_two) * grad_wide * grad_wide
    moment_hat = new_moment / (1.0 - beta_one**step_count)
    second_hat = new_second / (1.0 - beta_two**step_count)
    new_master = master - learn_rate * (
        moment_hat / (jnp.sqrt(second_hat) + adam_eps) + weight_decay * master
    )
    return (new_master, new_moment, new_second)


def move(array, target):
    pairs = []
    for source in range(128):
        rest, coords = source, []
        for size in reversed(SIZES):
            rest, coord = divmod(rest, size)
            coords.append(coord)
        index = 0
        for coord, size in zip(target(*reversed(coords)), SIZES):
            index = index * size + coord % size
        pairs.append((source, index))
    return lax.ppermute(array, AXES, pairs)


def to_sibling(array):
    return move(array, lambda z, xl, c, y, xh: (z, xl, 1 - c, y, xh))


def transpose(array):
    return move(array, lambda z, xl, c, y, xh: (y, xh, c, z, xl))


def dot(a, b):
    return jnp.dot(a, b, preferred_element_type=jnp.float32)


def params(mib):
    return pltpu.CompilerParams(vmem_limit_bytes=mib * MIB)


VMEM = pl.BlockSpec(memory_space=pltpu.VMEM)
SMEM = pl.BlockSpec(memory_space=pltpu.SMEM)
ANY = pl.BlockSpec(memory_space=pl.ANY)


def select_rows(slots, rows):
    hot = lax.broadcasted_iota(jnp.int32, (slots.shape[0], rows), 1) == slots
    return hot.astype(jnp.bfloat16)


def order_kernel(slots_ref, x_ref, out_ref):
    hot = select_rows(slots_ref[...], x_ref.shape[0])
    out_ref[...] = dot(hot, x_ref[...]).astype(jnp.bfloat16)


def own_kernel(slots_ref, x_ref, w_ref, out_ref):
    hot = select_rows(slots_ref[...], x_ref.shape[0])
    half = x_ref.shape[1] // STEPS
    for step in range(STEPS):
        ordered = dot(hot, x_ref[:, step * half : (step + 1) * half]).astype(jnp.bfloat16)
        out_ref[step] = dot(ordered, w_ref[...])


def add_kernel(own_ref, x_ref, w_ref, cos_ref, sin_ref, len_ref, after_ref, out_ref):
    del cos_ref, sin_ref, len_ref, after_ref
    half = x_ref.shape[1] // STEPS
    for step in range(STEPS):
        total = own_ref[step] + dot(x_ref[:, step * half : (step + 1) * half], w_ref[...])
        total = total.astype(jnp.bfloat16)
        for chip in range(8):
            out_ref[chip, step * SLOTS : (step + 1) * SLOTS, :] = total[
                chip * SLOTS : (chip + 1) * SLOTS
            ]


CHUNKS = 2
PER = SLOTS // CHUNKS
ROWS = STEPS * GROUP


def attend_kernel(
    parts_ref, cos_ref, sin_ref, len_ref, key_buf, value_buf, out_ref,
    q_buf, kx_buf, vx_buf, mix_buf, att_buf,
):
    total = parts_ref[0].astype(jnp.float32)
    for chip in range(1, 8):
        total = total + parts_ref[chip].astype(jnp.float32)
    cosine = cos_ref[...]
    sine = sin_ref[...]

    def rotate(vectors):
        turned = vectors * cosine + pltpu.roll(vectors, HEAD // 2, 1) * sine
        return turned.astype(jnp.bfloat16).astype(jnp.float32)

    for head in range(GROUP):
        turned = rotate(total[:, head * HEAD : (head + 1) * HEAD])
        for step in range(STEPS):
            q_buf[pl.ds(step * GROUP + head, SLOTS, stride=ROWS), :] = turned[
                step * SLOTS : (step + 1) * SLOTS
            ]
    k_new = rotate(total[:, GROUP * HEAD : (GROUP + 1) * HEAD])
    v_new = total[:, (GROUP + 1) * HEAD :].astype(jnp.bfloat16).astype(jnp.float32)
    for step in range(STEPS):
        for row in range(ROWS):
            kx_buf[step, pl.ds(row, SLOTS, stride=ROWS), :] = k_new[
                step * SLOTS : (step + 1) * SLOTS
            ]
            vx_buf[step, pl.ds(row, SLOTS, stride=ROWS), :] = v_new[
                step * SLOTS : (step + 1) * SLOTS
            ]
    scale = 1.0 / HEAD**0.5
    many = PER * ROWS
    for chunk in range(CHUNKS):
        first = chunk * many
        q_rows = q_buf[first : first + many]
        new_zero = jnp.sum(q_rows * kx_buf[0, first : first + many], axis=-1, keepdims=True) * scale
        new_one = jnp.sum(q_rows * kx_buf[1, first : first + many], axis=-1, keepdims=True) * scale
        row = lax.broadcasted_iota(jnp.int32, (many, 1), 0)
        second_step = lax.rem(row, ROWS) >= GROUP
        new_one = jnp.where(second_step, new_one, -1e30)
        scores = []
        for slot in range(PER):
            scores.append(
                lax.dot_general(
                    q_rows[slot * ROWS : (slot + 1) * ROWS].astype(jnp.bfloat16),
                    key_buf[chunk * PER + slot],
                    (((1,), (1,)), ((), ())),
                    preferred_element_type=jnp.float32,
                )
            )
        scores = jnp.concatenate(scores, axis=0) * scale
        position = lax.broadcasted_iota(jnp.int32, (many, CACHE), 1)
        scores = jnp.where(position < len_ref[first : first + many], scores, -1e30)
        top = jnp.maximum(
            jnp.max(scores, axis=-1, keepdims=True), jnp.maximum(new_zero, new_one)
        )
        scores = jnp.exp(scores - top)
        new_zero = jnp.exp(new_zero - top)
        new_one = jnp.exp(new_one - top)
        total_exp = jnp.sum(scores, axis=-1, keepdims=True) + new_zero + new_one
        scores = scores / total_exp
        new_zero = (new_zero / total_exp).astype(jnp.bfloat16).astype(jnp.float32)
        new_one = (new_one / total_exp).astype(jnp.bfloat16).astype(jnp.float32)
        mixed = []
        for slot in range(PER):
            mixed.append(
                dot(
                    scores[slot * ROWS : (slot + 1) * ROWS].astype(jnp.bfloat16),
                    value_buf[chunk * PER + slot],
                )
            )
        mixed = jnp.concatenate(mixed, axis=0)
        mixed = mixed + new_zero * vx_buf[0, first : first + many]
        mixed = mixed + new_one * vx_buf[1, first : first + many]
        mix_buf[first : first + many] = mixed
    for head in range(GROUP):
        for step in range(STEPS):
            att_buf[head, pl.ds(step, SLOTS, stride=STEPS), :] = mix_buf[
                pl.ds(step * GROUP + head, SLOTS, stride=ROWS), :
            ]
    for head in range(GROUP):
        part = att_buf[head].astype(jnp.bfloat16)
        for chip in range(8):
            out_ref[chip, :, head * HEAD : (head + 1) * HEAD] = part


def attend(parts, cosine, sine, lengths, keys, values):
    flat = SLOTS * ROWS
    return pl.pallas_call(
        attend_kernel,
        out_shape=jax.ShapeDtypeStruct((8, STEPS * SLOTS, GROUP * HEAD), jnp.bfloat16),
        in_specs=[VMEM] * 6,
        out_specs=VMEM,
        scratch_shapes=[
            pltpu.VMEM((flat, HEAD), jnp.float32),
            pltpu.VMEM((STEPS, flat, HEAD), jnp.float32),
            pltpu.VMEM((STEPS, flat, HEAD), jnp.float32),
            pltpu.VMEM((flat, HEAD), jnp.float32),
            pltpu.VMEM((GROUP, STEPS * SLOTS, HEAD), jnp.float32),
        ],
        compiler_params=params(12),
    )(parts, cosine, sine, lengths, keys, values)


def out_kernel(core_ref, att_ref, own_ref, sibling_ref, out_ref):
    core = core_ref[0]
    for w_ref, half in ((own_ref, core), (sibling_ref, 1 - core)):
        product = dot(att_ref[...], w_ref[...]).astype(jnp.bfloat16)
        columns = pl.ds(pl.multiple_of(half * 512, 512), 512)
        for chip in range(8):
            out_ref[chip, :, columns] = product[chip * 64 : (chip + 1) * 64]


def project(core, att, own, sibling):
    return pl.pallas_call(
        out_kernel,
        out_shape=jax.ShapeDtypeStruct((8, 64, 1024), jnp.bfloat16),
        in_specs=[SMEM, VMEM, VMEM, VMEM],
        out_specs=VMEM,
        compiler_params=params(16),
    )(core, att, own, sibling)


def per_device(
    tokens_x,
    slot_rows,
    cache_keys,
    cache_values,
    lengths,
    master_query,
    moment_query,
    second_query,
    gradient_query,
    master_keyval,
    moment_keyval,
    second_keyval,
    gradient_keyval,
    master_output,
    moment_output,
    second_output,
    gradient_output,
):
    core = lax.axis_index("c")

    x_own = tokens_x.reshape(64, 1024)
    x_all = lax.all_to_all(
        jnp.broadcast_to(x_own[None], (8, 64, 1024)), TP, 0, 0, tiled=True
    ).reshape(512, 1024)

    state_output = adam_step(master_output, moment_output, second_output, gradient_output)
    w_output = state_output[0].astype(jnp.bfloat16)
    state_query = adam_step(master_query, moment_query, second_query, gradient_query)
    state_keyval = adam_step(master_keyval, moment_keyval, second_keyval, gradient_keyval)
    w_own = jnp.concatenate(
        [
            state_query[0].astype(jnp.bfloat16),
            state_keyval[0].astype(jnp.bfloat16).reshape(512, 256),
        ],
        axis=1,
    )
    w_own, w_output = lax.optimization_barrier((w_own, w_output))
    w_sibling = to_sibling(w_own)
    w_output_sibling = to_sibling(w_output)

    by_core = slot_rows.reshape(8, 2, SLOTS).transpose(1, 0, 2).reshape(2, 256, 1)
    mine = lax.dynamic_index_in_dim(by_core, core, 0, False)
    others = lax.dynamic_index_in_dim(by_core, 1 - core, 0, False)
    x_send = pl.pallas_call(
        order_kernel,
        out_shape=jax.ShapeDtypeStruct((256, 1024), jnp.bfloat16),
        in_specs=[VMEM] * 2,
        out_specs=VMEM,
        compiler_params=params(16),
    )(others, x_all)
    x_sibling = to_sibling(x_send)
    own = pl.pallas_call(
        own_kernel,
        out_shape=jax.ShapeDtypeStruct((STEPS, 256, 768), jnp.float32),
        in_specs=[VMEM] * 3,
        out_specs=VMEM,
        compiler_params=params(16),
    )(mine, x_all, w_own)
    positions = (
        jnp.arange(STEPS, dtype=jnp.int32)[:, None] + lengths[None, :]
    ).reshape(STEPS * SLOTS, 1)
    freqs = rope_base ** (-2.0 * jnp.arange(HEAD // 2, dtype=jnp.float32) / HEAD)
    angles = positions.astype(jnp.float32) * freqs
    cosine = jnp.cos(angles)
    sine = jnp.sin(angles)
    cosine = jnp.concatenate([cosine, cosine], axis=1)
    sine = jnp.concatenate([-sine, sine], axis=1)
    length_rows = jnp.repeat(lengths, ROWS)[:, None]
    parts = pl.pallas_call(
        add_kernel,
        out_shape=jax.ShapeDtypeStruct((8, STEPS * SLOTS, 768), jnp.bfloat16),
        in_specs=[VMEM] * 6 + [ANY],
        out_specs=VMEM,
        compiler_params=params(16),
    )(own, x_sibling, w_sibling, cosine, sine, length_rows, w_output_sibling)
    parts = lax.all_to_all(parts, CHIPS, 0, 0, tiled=True)

    attended = attend(
        parts,
        cosine,
        sine,
        length_rows,
        cache_keys.reshape(SLOTS, CACHE, HEAD),
        cache_values.reshape(SLOTS, CACHE, HEAD),
    )
    attended = lax.all_to_all(attended, CHIPS, 0, 0, tiled=True).reshape(512, 512)
    partial_out = project(core.reshape(1), attended, w_output, w_output_sibling)
    partial_out = lax.all_to_all(partial_out, TP, 0, 0, tiled=True)
    decoded = jnp.sum(partial_out.astype(jnp.float32), axis=0).astype(jnp.bfloat16)
    decoded = transpose(decoded).reshape(SLOTS, STEPS, 1024)
    return (
        state_query[0],
        state_query[1],
        state_query[2],
        state_keyval[0],
        state_keyval[1],
        state_keyval[2],
        state_output[0],
        state_output[1],
        state_output[2],
        decoded,
    )


def solution(mesh):
    fine = Mesh(mesh.devices.reshape(SIZES), AXES)
    rep = ("z", "xl", "c")
    tp = TP
    return jax.shard_map(
        per_device,
        mesh=fine,
        in_specs=(
            P(tp, None, rep),
            P(),
            P(rep, tp, None, None),
            P(rep, tp, None, None),
            P(rep),
            P(rep, tp),
            P(rep, tp),
            P(rep, tp),
            P(rep, tp),
            P(rep, None, tp),
            P(rep, None, tp),
            P(rep, None, tp),
            P(rep, None, tp),
            P(tp, rep),
            P(tp, rep),
            P(tp, rep),
            P(tp, rep),
        ),
        out_specs=(
            P(rep, tp),
            P(rep, tp),
            P(rep, tp),
            P(rep, None, tp),
            P(rep, None, tp),
            P(rep, None, tp),
            P(tp, rep),
            P(tp, rep),
            P(tp, rep),
            P(rep, None, tp),
        ),
        check_vma=False,
    )
```

```python
import functools

import jax
import jax.numpy as jnp
from jax import lax
from jax.experimental import pallas as pl
from jax.experimental.pallas import tpu as pltpu
from jax.sharding import Mesh, PartitionSpec as P

learn_rate = 0.002
beta_one = 0.9
beta_two = 0.95
adam_eps = 1e-08
weight_decay = 0.1
step_count = 100.0
rope_base = 500000.0

AXES = ("z", "xl", "c", "y", "xh")
SIZES = (4, 2, 2, 4, 2)
CHIPS = ("z", "xl")
TP = ("y", "xh")
STEPS = 2
SLOTS = 32
CACHE = 384
HEAD = 128
GROUP = 4
MIB = 1024 * 1024


def adam_step(master, moment, second, gradient):
    grad_wide = gradient.astype(jnp.float32)
    new_moment = beta_one * moment + (1.0 - beta_one) * grad_wide
    new_second = beta_two * second + (1.0 - beta_two) * grad_wide * grad_wide
    moment_hat = new_moment / (1.0 - beta_one**step_count)
    second_hat = new_second / (1.0 - beta_two**step_count)
    new_master = master - learn_rate * (
        moment_hat / (jnp.sqrt(second_hat) + adam_eps) + weight_decay * master
    )
    return (new_master, new_moment, new_second)


def move(array, target):
    pairs = []
    for source in range(128):
        rest, coords = source, []
        for size in reversed(SIZES):
            rest, coord = divmod(rest, size)
            coords.append(coord)
        index = 0
        for coord, size in zip(target(*reversed(coords)), SIZES):
            index = index * size + coord % size
        pairs.append((source, index))
    return lax.ppermute(array, AXES, pairs)


def to_sibling(array):
    return move(array, lambda z, xl, c, y, xh: (z, xl, 1 - c, y, xh))


def transpose(array):
    return move(array, lambda z, xl, c, y, xh: (y, xh, c, z, xl))


def dot(a, b):
    return jnp.dot(a, b, preferred_element_type=jnp.float32)


def params(mib):
    return pltpu.CompilerParams(vmem_limit_bytes=mib * MIB)


VMEM = pl.BlockSpec(memory_space=pltpu.VMEM)
SMEM = pl.BlockSpec(memory_space=pltpu.SMEM)
ANY = pl.BlockSpec(memory_space=pl.ANY)


def select_rows(slots, rows):
    hot = lax.broadcasted_iota(jnp.int32, (slots.shape[0], rows), 1) == slots
    return hot.astype(jnp.bfloat16)


def order_kernel(slots_ref, x_ref, out_ref):
    hot = select_rows(slots_ref[...], x_ref.shape[0])
    out_ref[...] = dot(hot, x_ref[...]).astype(jnp.bfloat16)


def own_kernel(slots_ref, x_ref, w_ref, out_ref):
    hot = select_rows(slots_ref[...], x_ref.shape[0])
    half = x_ref.shape[1] // STEPS
    for step in range(STEPS):
        ordered = dot(hot, x_ref[:, step * half : (step + 1) * half]).astype(jnp.bfloat16)
        out_ref[step] = dot(ordered, w_ref[...])


def add_kernel(own_ref, x_ref, w_ref, cos_ref, sin_ref, len_ref, after_ref, out_ref):
    del cos_ref, sin_ref, len_ref, after_ref
    half = x_ref.shape[1] // STEPS
    for step in range(STEPS):
        total = own_ref[step] + dot(x_ref[:, step * half : (step + 1) * half], w_ref[...])
        total = total.astype(jnp.bfloat16)
        for chip in range(8):
            out_ref[chip, step * SLOTS : (step + 1) * SLOTS, :] = total[
                chip * SLOTS : (chip + 1) * SLOTS
            ]


CHUNKS = 2
PER = SLOTS // CHUNKS
ROWS = STEPS * GROUP


def attend_kernel(
    parts_ref, cos_ref, sin_ref, len_ref, key_buf, value_buf, out_ref,
    q_buf, kx_buf, vx_buf, mix_buf, att_buf,
):
    total = parts_ref[0].astype(jnp.float32)
    for chip in range(1, 8):
        total = total + parts_ref[chip].astype(jnp.float32)
    cosine = cos_ref[...]
    sine = sin_ref[...]

    def rotate(vectors):
        turned = vectors * cosine + pltpu.roll(vectors, HEAD // 2, 1) * sine
        return turned.astype(jnp.bfloat16).astype(jnp.float32)

    for head in range(GROUP):
        turned = rotate(total[:, head * HEAD : (head + 1) * HEAD])
        for step in range(STEPS):
            q_buf[pl.ds(step * GROUP + head, SLOTS, stride=ROWS), :] = turned[
                step * SLOTS : (step + 1) * SLOTS
            ]
    k_new = rotate(total[:, GROUP * HEAD : (GROUP + 1) * HEAD])
    v_new = total[:, (GROUP + 1) * HEAD :].astype(jnp.bfloat16).astype(jnp.float32)
    for step in range(STEPS):
        for row in range(ROWS):
            kx_buf[step, pl.ds(row, SLOTS, stride=ROWS), :] = k_new[
                step * SLOTS : (step + 1) * SLOTS
            ]
            vx_buf[step, pl.ds(row, SLOTS, stride=ROWS), :] = v_new[
                step * SLOTS : (step + 1) * SLOTS
            ]
    scale = 1.0 / HEAD**0.5
    many = PER * ROWS
    for chunk in range(CHUNKS):
        first = chunk * many
        q_rows = q_buf[first : first + many]
        new_zero = jnp.sum(q_rows * kx_buf[0, first : first + many], axis=-1, keepdims=True) * scale
        new_one = jnp.sum(q_rows * kx_buf[1, first : first + many], axis=-1, keepdims=True) * scale
        row = lax.broadcasted_iota(jnp.int32, (many, 1), 0)
        second_step = lax.rem(row, ROWS) >= GROUP
        new_one = jnp.where(second_step, new_one, -1e30)
        scores = []
        for slot in range(PER):
            scores.append(
                lax.dot_general(
                    q_rows[slot * ROWS : (slot + 1) * ROWS].astype(jnp.bfloat16),
                    key_buf[chunk * PER + slot],
                    (((1,), (1,)), ((), ())),
                    preferred_element_type=jnp.float32,
                )
            )
        scores = jnp.concatenate(scores, axis=0) * scale
        position = lax.broadcasted_iota(jnp.int32, (many, CACHE), 1)
        scores = jnp.where(position < len_ref[first : first + many], scores, -1e30)
        top = jnp.maximum(
            jnp.max(scores, axis=-1, keepdims=True), jnp.maximum(new_zero, new_one)
        )
        scores = jnp.exp(scores - top)
        new_zero = jnp.exp(new_zero - top)
        new_one = jnp.exp(new_one - top)
        total_exp = jnp.sum(scores, axis=-1, keepdims=True) + new_zero + new_one
        scores = scores / total_exp
        new_zero = (new_zero / total_exp).astype(jnp.bfloat16).astype(jnp.float32)
        new_one = (new_one / total_exp).astype(jnp.bfloat16).astype(jnp.float32)
        mixed = []
        for slot in range(PER):
            mixed.append(
                dot(
                    scores[slot * ROWS : (slot + 1) * ROWS].astype(jnp.bfloat16),
                    value_buf[chunk * PER + slot],
                )
            )
        mixed = jnp.concatenate(mixed, axis=0)
        mixed = mixed + new_zero * vx_buf[0, first : first + many]
        mixed = mixed + new_one * vx_buf[1, first : first + many]
        mix_buf[first : first + many] = mixed
    for head in range(GROUP):
        for step in range(STEPS):
            att_buf[head, pl.ds(step, SLOTS, stride=STEPS), :] = mix_buf[
                pl.ds(step * GROUP + head, SLOTS, stride=ROWS), :
            ]
    for head in range(GROUP):
        part = att_buf[head].astype(jnp.bfloat16)
        for chip in range(8):
            out_ref[chip, :, head * HEAD : (head + 1) * HEAD] = part


def attend(parts, cosine, sine, lengths, keys, values):
    flat = SLOTS * ROWS
    return pl.pallas_call(
        attend_kernel,
        out_shape=jax.ShapeDtypeStruct((8, STEPS * SLOTS, GROUP * HEAD), jnp.bfloat16),
        in_specs=[VMEM] * 6,
        out_specs=VMEM,
        scratch_shapes=[
            pltpu.VMEM((flat, HEAD), jnp.float32),
            pltpu.VMEM((STEPS, flat, HEAD), jnp.float32),
            pltpu.VMEM((STEPS, flat, HEAD), jnp.float32),
            pltpu.VMEM((flat, HEAD), jnp.float32),
            pltpu.VMEM((GROUP, STEPS * SLOTS, HEAD), jnp.float32),
        ],
        compiler_params=params(12),
    )(parts, cosine, sine, lengths, keys, values)


def out_kernel(core_ref, att_ref, own_ref, sibling_ref, out_ref):
    core = core_ref[0]
    for w_ref, half in ((own_ref, core), (sibling_ref, 1 - core)):
        product = dot(att_ref[...], w_ref[...]).astype(jnp.bfloat16)
        columns = pl.ds(pl.multiple_of(half * 512, 512), 512)
        for chip in range(8):
            out_ref[chip, :, columns] = product[chip * 64 : (chip + 1) * 64]


def project(core, att, own, sibling):
    return pl.pallas_call(
        out_kernel,
        out_shape=jax.ShapeDtypeStruct((8, 64, 1024), jnp.bfloat16),
        in_specs=[SMEM, VMEM, VMEM, VMEM],
        out_specs=VMEM,
        compiler_params=params(16),
    )(core, att, own, sibling)


def per_device(
    tokens_x,
    slot_rows,
    cache_keys,
    cache_values,
    lengths,
    master_query,
    moment_query,
    second_query,
    gradient_query,
    master_keyval,
    moment_keyval,
    second_keyval,
    gradient_keyval,
    master_output,
    moment_output,
    second_output,
    gradient_output,
):
    core = lax.axis_index("c")

    x_own = tokens_x.reshape(64, 1024)
    x_all = lax.all_to_all(
        jnp.broadcast_to(x_own[None], (8, 64, 1024)), TP, 0, 0, tiled=True
    ).reshape(512, 1024)

    state_output = adam_step(master_output, moment_output, second_output, gradient_output)
    w_output = state_output[0].astype(jnp.bfloat16)
    state_query = adam_step(master_query, moment_query, second_query, gradient_query)
    state_keyval = adam_step(master_keyval, moment_keyval, second_keyval, gradient_keyval)
    w_own = jnp.concatenate(
        [
            state_query[0].astype(jnp.bfloat16),
            state_keyval[0].astype(jnp.bfloat16).reshape(512, 256),
        ],
        axis=1,
    )
    positions = (
        jnp.arange(STEPS, dtype=jnp.int32)[:, None] + lengths[None, :]
    ).reshape(STEPS * SLOTS, 1)
    freqs = rope_base ** (-2.0 * jnp.arange(HEAD // 2, dtype=jnp.float32) / HEAD)
    angles = positions.astype(jnp.float32) * freqs
    cosine = jnp.cos(angles)
    sine = jnp.sin(angles)
    cosine = jnp.concatenate([cosine, cosine], axis=1)
    sine = jnp.concatenate([-sine, sine], axis=1)
    length_rows = jnp.repeat(lengths, ROWS)[:, None]
    by_core = slot_rows.reshape(8, 2, SLOTS).transpose(1, 0, 2).reshape(2, 256, 1)
    mine = lax.dynamic_index_in_dim(by_core, core, 0, False)
    others = lax.dynamic_index_in_dim(by_core, 1 - core, 0, False)
    w_own, w_output, cosine, sine, length_rows, mine, others = lax.optimization_barrier(
        (w_own, w_output, cosine, sine, length_rows, mine, others)
    )
    w_sibling = to_sibling(w_own)
    w_output_sibling = to_sibling(w_output)

    x_send = pl.pallas_call(
        order_kernel,
        out_shape=jax.ShapeDtypeStruct((256, 1024), jnp.bfloat16),
        in_specs=[VMEM] * 2,
        out_specs=VMEM,
        compiler_params=params(16),
    )(others, x_all)
    x_sibling = to_sibling(x_send)
    own = pl.pallas_call(
        own_kernel,
        out_shape=jax.ShapeDtypeStruct((STEPS, 256, 768), jnp.float32),
        in_specs=[VMEM] * 3,
        out_specs=VMEM,
        compiler_params=params(16),
    )(mine, x_all, w_own)
    parts = pl.pallas_call(
        add_kernel,
        out_shape=jax.ShapeDtypeStruct((8, STEPS * SLOTS, 768), jnp.bfloat16),
        in_specs=[VMEM] * 6 + [ANY],
        out_specs=VMEM,
        compiler_params=params(16),
    )(own, x_sibling, w_sibling, cosine, sine, length_rows, w_output_sibling)
    parts = lax.all_to_all(parts, CHIPS, 0, 0, tiled=True)

    attended = attend(
        parts,
        cosine,
        sine,
        length_rows,
        cache_keys.reshape(SLOTS, CACHE, HEAD),
        cache_values.reshape(SLOTS, CACHE, HEAD),
    )
    attended = lax.all_to_all(attended, CHIPS, 0, 0, tiled=True).reshape(512, 512)
    partial_out = project(core.reshape(1), attended, w_output, w_output_sibling)
    partial_out = lax.all_to_all(partial_out, TP, 0, 0, tiled=True)
    decoded = jnp.sum(partial_out.astype(jnp.float32), axis=0).astype(jnp.bfloat16)
    decoded = transpose(decoded).reshape(SLOTS, STEPS, 1024)
    return (
        state_query[0],
        state_query[1],
        state_query[2],
        state_keyval[0],
        state_keyval[1],
        state_keyval[2],
        state_output[0],
        state_output[1],
        state_output[2],
        decoded,
    )


def solution(mesh):
    fine = Mesh(mesh.devices.reshape(SIZES), AXES)
    rep = ("z", "xl", "c")
    tp = TP
    return jax.shard_map(
        per_device,
        mesh=fine,
        in_specs=(
            P(tp, None, rep),
            P(),
            P(rep, tp, None, None),
            P(rep, tp, None, None),
            P(rep),
            P(rep, tp),
            P(rep, tp),
            P(rep, tp),
            P(rep, tp),
            P(rep, None, tp),
            P(rep, None, tp),
            P(rep, None, tp),
            P(rep, None, tp),
            P(tp, rep),
            P(tp, rep),
            P(tp, rep),
            P(tp, rep),
        ),
        out_specs=(
            P(rep, tp),
            P(rep, tp),
            P(rep, tp),
            P(rep, None, tp),
            P(rep, None, tp),
            P(rep, None, tp),
            P(tp, rep),
            P(tp, rep),
            P(tp, rep),
            P(rep, None, tp),
        ),
        check_vma=False,
    )
```
